128 devices in a mesh: pb: 8 (over x, core), kv: 16 (over y, z).
Axes of the slice: x: 4, y: 4, z: 4, core: 2. Of those that a mesh axis runs over, the one named last changes fastest.
Arguments:
- packed_query_rows: bfloat16 [49152, 4096], P(('pb', 'kv')), as said below
- packed_key_rows: bfloat16 [49152, 1024], P(('pb', 'kv')), as said below
- packed_value_rows: bfloat16 [49152, 1024], P(('pb', 'kv')), may hold values from -6 to 6
- doc_lengths: int32 [12], replicated, may hold values from 1 to 6144, 49152 in all
Outputs:
- attended: bfloat16 [49152, 4096], P(('pb', 'kv'))
The draws below stay inside these ranges and needn't reach their ends.
Inputs may be any that keep to these rules, and one draw needn't show every extreme that they name: `packed_query_rows`: queries of the shown draw are of order one; a few rows may be much larger. `packed_key_rows`: keys of the shown draw are of order one; a few rows may be much larger. `doc_lengths`: the longest document has exactly 6144 tokens.
All inputs are finite; a program needn't handle non-finite values.
Results may differ from the reference program's by a relative error of at most 0.0065.
Values may be sent and summed in bfloat16 or wider, within the bound.
No kernel may reach another device: no remote copies, remote signals or barrier semaphores. Data moves between devices by JAX's collectives and lax.ppermute only.
A program may use at most 192 MiB of HBM per device.

```python
import math
import jax
import jax.numpy as jnp
import numpy as np
from jax import lax

QUERY_HEADS = 32
KEY_VALUE_HEADS = 8
HEAD_WIDTH = 128
PACKED_TOKENS = 49152
MOST = 6144
DOCS = 12


def draw_packed_query_rows(key, part):
    key = jax.random.fold_in(key, 11)
    first = jax.random.fold_in(key, 0)
    offset_start = jax.random.normal(first, (PACKED_TOKENS, QUERY_HEADS, HEAD_WIDTH), jnp.float32)
    return jnp.clip(offset_start, -8.0, 8.0).reshape(PACKED_TOKENS, QUERY_HEADS * HEAD_WIDTH).astype(jnp.bfloat16)


def draw_packed_key_rows(key, part):
    key = jax.random.fold_in(key, 23)
    offset_start = jax.random.normal(key, (PACKED_TOKENS, KEY_VALUE_HEADS, HEAD_WIDTH), jnp.float32)
    return jnp.clip(offset_start, -8.0, 8.0).reshape(PACKED_TOKENS, KEY_VALUE_HEADS * HEAD_WIDTH).astype(jnp.bfloat16)


def block_levels(stream_key, extent, cuts, smallest, high):
    level = 1.0
    for dim, shards_of in cuts:
        draws = jax.random.uniform(jax.random.fold_in(jax.random.fold_in(stream_key, 6), dim), (shards_of,), jnp.float32, smallest / len(cuts), high / len(cuts))
        level = level * jnp.repeat(jnp.exp(draws), extent[dim] // shards_of).reshape((-1,) + (1,) * (len(extent) - 1 - dim))
    return level


def split_up(amount, total, bound, slope):
    loads = [(1 << 20) // math.isqrt(grade ** slope) + 1 for grade in range(2, amount + 1)]
    spare, counts = total - bound - (amount - 1), [1] * (amount - 1)
    while spare > 0:
        movable = [i for i in range(amount - 1) if counts[i] < bound]
        pool, left = sum([loads[i] for i in movable]), spare
        for i in movable:
            addition = min(bound - counts[i], max(1, left * loads[i] // pool), spare)
            counts[i] = counts[i] + addition
            spare = spare - addition
    return np.array([bound] + counts)


def ragged(key, count, total, limit, skew):
    if count == 2:
        one = jax.random.randint(key, (), max(1, total - limit), min(limit, total - 1) + 1)
        return jnp.stack([one, total - one])
    lengths = jnp.asarray(split_up(count, total, limit, skew), jnp.int32)
    twos = (count - 1) // 2
    giver, receiver = lengths[1:1 + 2 * twos:2], lengths[2:2 + 2 * twos:2]
    margin = jnp.minimum(giver - 1, limit - receiver)
    shifted = jax.random.randint(jax.random.fold_in(key, 1), (twos,), 0, 1 << 20) % (margin + 1)
    lengths = lengths.at[1:1 + 2 * twos:2].set(giver - shifted).at[2:2 + 2 * twos:2].set(receiver + shifted)
    return lengths[jax.random.permutation(jax.random.fold_in(key, 2), count)]


def noise(stream_key, shape, scale, limit, cuts=(), kind=jnp.bfloat16):
    values = jax.random.normal(stream_key, shape, jnp.float32) * scale
    if len(cuts) > 0:
        values = block_levels(stream_key, shape, cuts, -0.22, 0.18) * values
    return jnp.clip(values, min=-limit, max=limit).astype(kind)


def setup_inputs(seed: int = 0) -> dict:
    arg_keys = jax.random.split(jax.random.key(seed), 5)
    packed_query_rows = draw_packed_query_rows(jax.random.fold_in(arg_keys[4], 71), 0)
    packed_key_rows = draw_packed_key_rows(jax.random.fold_in(arg_keys[4], 71), 0)
    packed_value_rows = noise(arg_keys[2], (PACKED_TOKENS, KEY_VALUE_HEADS * HEAD_WIDTH), 1.0, 6.0, ((0, 128),))
    doc_lengths = ragged(arg_keys[3], DOCS, PACKED_TOKENS, MOST, 2).astype(jnp.int32)
    return dict(packed_query_rows=packed_query_rows, packed_key_rows=packed_key_rows, packed_value_rows=packed_value_rows, doc_lengths=doc_lengths)


causal_score = -1e+30

def reference(packed_query_rows, packed_key_rows, packed_value_rows, doc_lengths):
    doc_ends = jnp.cumsum(doc_lengths).astype(jnp.int32)
    positions = jnp.arange(PACKED_TOKENS, dtype=jnp.int32)
    doc_ids = lax.optimization_barrier(jnp.sum((positions[:, None] >= doc_ends[None, :]).astype(jnp.int32), axis=1)).astype(jnp.int32)
    rows_per_block = 256
    leading_edge = MOST
    visible_span = leading_edge + rows_per_block
    query_group_width = QUERY_HEADS // KEY_VALUE_HEADS
    scaling = 1.0 / math.sqrt(HEAD_WIDTH)
    padded_keys = jnp.concatenate([jnp.zeros((leading_edge, KEY_VALUE_HEADS * HEAD_WIDTH), packed_key_rows.dtype), packed_key_rows], axis=0)
    padded_values = jnp.concatenate([jnp.zeros((leading_edge, KEY_VALUE_HEADS * HEAD_WIDTH), packed_value_rows.dtype), packed_value_rows], axis=0)
    pad_docs = jnp.concatenate([jnp.full((leading_edge,), -1, jnp.int32), doc_ids], axis=0)
    pad_pos = jnp.concatenate([jnp.arange(leading_edge, dtype=jnp.int32) - leading_edge, positions], axis=0)

    def one_block(block_index):
        first_position = (block_index * rows_per_block).astype(jnp.int32)
        query_block = lax.dynamic_slice_in_dim(packed_query_rows, first_position, rows_per_block, 0).astype(jnp.float32)
        query_block = query_block.reshape(rows_per_block, KEY_VALUE_HEADS, query_group_width, HEAD_WIDTH)
        local_keys = lax.dynamic_slice_in_dim(padded_keys, first_position, visible_span, 0).astype(jnp.float32).reshape(visible_span, KEY_VALUE_HEADS, HEAD_WIDTH)
        local_values = lax.dynamic_slice_in_dim(padded_values, first_position, visible_span, 0).astype(jnp.float32).reshape(visible_span, KEY_VALUE_HEADS, HEAD_WIDTH)
        key_doc = lax.dynamic_slice_in_dim(pad_docs, first_position, visible_span, 0)
        key_pos = lax.dynamic_slice_in_dim(pad_pos, first_position, visible_span, 0)
        query_doc = lax.dynamic_slice_in_dim(doc_ids, first_position, rows_per_block, 0)
        query_pos = lax.dynamic_slice_in_dim(positions, first_position, rows_per_block, 0)
        scores = jnp.einsum('qgrd,kgd->grqk', query_block, local_keys) * scaling
        allowed = (key_doc[None, :] == query_doc[:, None]) & (key_pos[None, :] <= query_pos[:, None])
        scores = jnp.where(allowed, scores, causal_score)
        largest = lax.optimization_barrier(jnp.max(scores, axis=-1, keepdims=True))
        weights = jnp.where(allowed, jnp.exp(scores - largest), 0.0)
        totals = lax.optimization_barrier(jnp.sum(weights, axis=-1))
        rounded = lax.optimization_barrier(weights.astype(jnp.bfloat16)).astype(jnp.float32)
        summed = jnp.einsum('grqk,kgd->qgrd', rounded, local_values)
        result = summed / totals.transpose(2, 0, 1)[..., None]
        return result.reshape(rows_per_block, QUERY_HEADS * HEAD_WIDTH).astype(jnp.bfloat16)
    blocks = lax.map(one_block, jnp.arange(PACKED_TOKENS // rows_per_block, dtype=jnp.int32))
    return blocks.reshape(PACKED_TOKENS, QUERY_HEADS * HEAD_WIDTH)
```

```python
import functools
import math

import jax
import jax.numpy as jnp
from jax import lax
from jax.experimental import pallas as pl
from jax.experimental.pallas import tpu as pltpu
from jax.sharding import PartitionSpec as P

QUERY_HEADS = 32
KEY_VALUE_HEADS = 8
HEAD_WIDTH = 128
DOCS = 12
CHUNKS = 2
TILE = 1024
STRIP = 256
WIDE = 1024
ONES = 16
GROUP = 4
LOG2_SCALE = math.log2(math.e) / math.sqrt(HEAD_WIDTH)
SAFE_EXPONENT = 96.0
LOW = -1e30
MASKED = -3e38
VMEM_LIMIT = 56 * 1024 * 1024


def first_doc(docs_ref, first):
    start, end = docs_ref[0], docs_ref[DOCS]
    for i in range(1, DOCS):
        inside = docs_ref[i] <= first
        start = jnp.where(inside, docs_ref[i], start)
        end = jnp.where(inside, docs_ref[DOCS + i], end)
    return start, end


def with_ones(vt):
    return jnp.concatenate([vt, jnp.ones((ONES, vt.shape[1]), vt.dtype)], axis=0)


def fast_step(qt_ref, k_ref, vt_ref, acc_ref, rows, first_key, width, allowed=None):
    keys = k_ref[pl.ds(first_key, width), :]
    scores = jnp.dot(keys, qt_ref[:, rows], preferred_element_type=jnp.float32)
    weights = jnp.exp2(scores * LOG2_SCALE)
    if allowed is not None:
        weights = jnp.where(allowed, weights, 0.0)
    acc_ref[:, rows] += jnp.dot(
        with_ones(vt_ref[:, pl.ds(first_key, width)]),
        weights.astype(jnp.bfloat16),
        preferred_element_type=jnp.float32,
    )


def safe_step(qt_ref, k_ref, vt_ref, acc_ref, max_ref, first_key, width, allowed):
    keys = k_ref[pl.ds(first_key, width), :]
    scores = jnp.dot(keys, qt_ref[...], preferred_element_type=jnp.float32)
    scores = jnp.where(allowed, scores * LOG2_SCALE, MASKED)
    old = max_ref[0:1, :]
    new = jnp.maximum(old, jnp.max(scores, axis=0, keepdims=True))
    weights = jnp.exp2(scores - new)
    factor = jnp.exp2(old - new)
    max_ref[...] = jnp.broadcast_to(new, max_ref.shape)
    acc_ref[...] = acc_ref[...] * factor + jnp.dot(
        with_ones(vt_ref[:, pl.ds(first_key, width)]),
        weights.astype(jnp.bfloat16),
        preferred_element_type=jnp.float32,
    )


def left_keys(qt_ref, k_ref, vt_ref, acc_ref, start, stop, active):
    low = start // STRIP * STRIP
    after = low + STRIP
    wide = jnp.maximum(stop - after, 0) // WIDE
    narrow = jnp.maximum(stop - after - wide * WIDE, 0) // STRIP
    groups = (active + STRIP - 1) // STRIP
    for count in range(1, TILE // STRIP + 1):

        @pl.when((start < stop) & (groups == count))
        def _():
            rows = slice(0, count * STRIP)
            place = lax.broadcasted_iota(jnp.int32, (STRIP, count * STRIP), 0)
            step = functools.partial(fast_step, qt_ref, k_ref, vt_ref, acc_ref, rows)
            step(pl.multiple_of(low, STRIP), STRIP, place >= start - low)
            for strips in range(1, WIDE // STRIP):

                @pl.when(narrow == strips)
                def _():
                    step(pl.multiple_of(after, STRIP), strips * STRIP)

            def one_wide(i, carry):
                step(pl.multiple_of(after + narrow * STRIP + i * WIDE, STRIP), WIDE)
                return carry

            lax.fori_loop(0, wide, one_wide, 0)


def row_starts(docs_ref, first):
    position = lax.broadcasted_iota(jnp.int32, (8, TILE), 1) + first
    start = jnp.full((8, TILE), docs_ref[0], jnp.int32)
    for i in range(1, DOCS):
        start = jnp.where(position >= docs_ref[i], docs_ref[i], start)
    return start


def safe_keys(qt_ref, k_ref, vt_ref, acc_ref, max_ref, starts, first, base, begin, end):
    def one(i, carry):
        first_key = pl.multiple_of(i * STRIP, STRIP)
        place = lax.broadcasted_iota(jnp.int32, (STRIP, TILE), 0) + (base + first_key)
        row = lax.broadcasted_iota(jnp.int32, (STRIP, TILE), 1) + first
        allowed = (place >= starts[0:1, :]) & (place <= row)
        safe_step(qt_ref, k_ref, vt_ref, acc_ref, max_ref, first_key, STRIP, allowed)
        return carry

    lax.fori_loop(begin, end, one, 0)


def attend_kernel(
    docs_ref, norm_ref, q_ref, k_ref, vt_ref, k_before_ref, vt_before_ref, o_ref, qt_ref, acc_ref, max_ref
):
    span = k_ref.shape[0]
    first = pl.program_id(0) * TILE
    start, end = first_doc(docs_ref, first)
    own_start = jnp.maximum(start, 0)
    before_start = jnp.minimum(jnp.maximum(start + span, 0), span)
    starts = row_starts(docs_ref, first)
    acc_ref[...] = jnp.zeros_like(acc_ref)
    qt = q_ref[...].astype(jnp.float32).T
    qt_ref[...] = qt.astype(qt_ref.dtype)
    largest = jnp.max(jnp.sum(qt * qt, axis=0, keepdims=True)) * norm_ref[0]
    bounded = largest <= (SAFE_EXPONENT / LOG2_SCALE) ** 2

    @pl.when(bounded)
    def _():
        active = jnp.minimum(end - first, TILE)
        left_keys(qt_ref, k_before_ref, vt_before_ref, acc_ref, before_start, span, active)
        left_keys(qt_ref, k_ref, vt_ref, acc_ref, own_start, first, active)

        @pl.when((start < first) & (end < first + TILE))
        def _():
            row = lax.broadcasted_iota(jnp.int32, acc_ref.shape, 1) + first
            acc_ref[...] = jnp.where(row < end, acc_ref[...], 0.0)

        for strip in range(TILE // STRIP):
            rows = slice(strip * STRIP, TILE)
            shape = (STRIP, TILE - strip * STRIP)
            place = lax.broadcasted_iota(jnp.int32, shape, 0)
            row = lax.broadcasted_iota(jnp.int32, shape, 1)
            allowed = (place <= row) & (place >= starts[0:1, rows] - (first + strip * STRIP))
            first_key = pl.multiple_of(first + strip * STRIP, STRIP)
            fast_step(qt_ref, k_ref, vt_ref, acc_ref, rows, first_key, STRIP, allowed)

    @pl.when(jnp.logical_not(bounded))
    def _():
        max_ref[...] = jnp.full_like(max_ref, LOW)
        safe_keys(
            qt_ref, k_before_ref, vt_before_ref, acc_ref, max_ref, starts, first, -span,
            before_start // STRIP, span // STRIP,
        )
        safe_keys(
            qt_ref, k_ref, vt_ref, acc_ref, max_ref, starts, first, 0,
            own_start // STRIP, (first + TILE) // STRIP,
        )

    result = acc_ref[0:HEAD_WIDTH, :] / acc_ref[HEAD_WIDTH : HEAD_WIDTH + 1, :]
    o_ref[...] = result.T.astype(o_ref.dtype)


def attend(docs, norm, q, k, vt, k_before, vt_before):
    span = q.shape[0]
    tile = pl.BlockSpec((TILE, HEAD_WIDTH), lambda t, *_: (t, 0))
    whole = lambda array: pl.BlockSpec(array.shape, lambda t, *_: (0, 0))
    pairs = span * span // 2
    return pl.pallas_call(
        attend_kernel,
        grid_spec=pltpu.PrefetchScalarGridSpec(
            num_scalar_prefetch=2,
            grid=(span // TILE,),
            in_specs=[tile, whole(k), whole(vt), whole(k_before), whole(vt_before)],
            out_specs=tile,
            scratch_shapes=[
                pltpu.VMEM((HEAD_WIDTH, TILE), jnp.bfloat16),
                pltpu.VMEM((HEAD_WIDTH + ONES, TILE), jnp.float32),
                pltpu.VMEM((8, TILE), jnp.float32),
            ],
        ),
        out_shape=jax.ShapeDtypeStruct((span, HEAD_WIDTH), jnp.bfloat16),
        compiler_params=pltpu.CompilerParams(vmem_limit_bytes=VMEM_LIMIT),
        cost_estimate=pl.CostEstimate(
            flops=pairs * 16 * HEAD_WIDTH, bytes_accessed=span * 1536, transcendentals=pairs
        ),
        name="attend",
    )(docs, norm, q, k, vt, k_before, vt_before)


def light_cost(*arrays):
    return pl.CostEstimate(
        flops=0, bytes_accessed=2 * sum(a.size * a.dtype.itemsize for a in arrays), transcendentals=0
    )


def pair_slots_kernel(copies, k_ref, v_ref, o_ref):
    for slot in range(GROUP):
        head = slice(slot // copies * HEAD_WIDTH, (slot // copies + 1) * HEAD_WIDTH)
        o_ref[slot, :, :HEAD_WIDTH] = k_ref[:, head]
        o_ref[slot, :, HEAD_WIDTH:] = v_ref[:, head]


def pair_slots(k, v, slots):
    rows = k.shape[0]
    copies = slots // KEY_VALUE_HEADS
    part = pl.BlockSpec((rows, GROUP // copies * HEAD_WIDTH), lambda t: (0, t))
    return pl.pallas_call(
        functools.partial(pair_slots_kernel, copies),
        grid=(slots // GROUP,),
        in_specs=[part, part],
        out_specs=pl.BlockSpec((GROUP, rows, 2 * HEAD_WIDTH), lambda t: (t, 0, 0)),
        out_shape=jax.ShapeDtypeStruct((slots, rows, 2 * HEAD_WIDTH), k.dtype),
        cost_estimate=light_cost(k, v),
        name="pair_slots",
    )(k, v)


def query_slots_kernel(q_ref, *o_refs):
    for slot in range(GROUP):
        for c, o_ref in enumerate(o_refs):
            head = slot * CHUNKS + c
            o_ref[slot] = q_ref[:, head * HEAD_WIDTH : (head + 1) * HEAD_WIDTH]


def query_slots(q, slots):
    rows = q.shape[0]
    return pl.pallas_call(
        query_slots_kernel,
        grid=(slots // GROUP,),
        in_specs=[pl.BlockSpec((rows, GROUP * CHUNKS * HEAD_WIDTH), lambda t: (0, t))],
        out_specs=[pl.BlockSpec((GROUP, rows, HEAD_WIDTH), lambda t: (t, 0, 0))] * CHUNKS,
        out_shape=[jax.ShapeDtypeStruct((slots, rows, HEAD_WIDTH), q.dtype)] * CHUNKS,
        cost_estimate=light_cost(q),
        name="query_slots",
    )(q)


def join_kernel(*refs):
    *parts, o_ref = refs
    for slot in range(GROUP):
        for c, part in enumerate(parts):
            head = slot * CHUNKS + c
            o_ref[:, head * HEAD_WIDTH : (head + 1) * HEAD_WIDTH] = part[slot]


def join(parts):
    slots, rows, _ = parts[0].shape
    return pl.pallas_call(
        join_kernel,
        grid=(slots // GROUP,),
        in_specs=[pl.BlockSpec((GROUP, rows, HEAD_WIDTH), lambda t: (t, 0, 0))] * CHUNKS,
        out_specs=pl.BlockSpec((rows, GROUP * CHUNKS * HEAD_WIDTH), lambda t: (0, t)),
        out_shape=jax.ShapeDtypeStruct((rows, slots * CHUNKS * HEAD_WIDTH), parts[0].dtype),
        cost_estimate=light_cost(*parts),
        name="join",
    )(*parts)


def prepare_kernel(kv_ref, k_ref, vt_ref, norm_ref):
    k = kv_ref[:, :HEAD_WIDTH]
    k_ref[...] = k
    vt_ref[...] = kv_ref[:, HEAD_WIDTH:].astype(jnp.float32).T.astype(vt_ref.dtype)
    kf = k.astype(jnp.float32)
    norm = jnp.full(norm_ref.shape, jnp.max(jnp.sum(kf * kf, axis=1, keepdims=True)), jnp.float32)

    @pl.when(pl.program_id(0) == 0)
    def _():
        norm_ref[...] = norm

    @pl.when(pl.program_id(0) > 0)
    def _():
        norm_ref[...] = jnp.maximum(norm_ref[...], norm)


def prepare(key_value):
    span = key_value.shape[0]
    return pl.pallas_call(
        prepare_kernel,
        grid=(span // TILE,),
        in_specs=[pl.BlockSpec((TILE, 2 * HEAD_WIDTH), lambda t: (t, 0))],
        out_specs=[
            pl.BlockSpec((TILE, HEAD_WIDTH), lambda t: (t, 0)),
            pl.BlockSpec((HEAD_WIDTH, TILE), lambda t: (0, t)),
            pl.BlockSpec((8, 128), lambda t: (0, 0)),
        ],
        out_shape=[
            jax.ShapeDtypeStruct((span, HEAD_WIDTH), key_value.dtype),
            jax.ShapeDtypeStruct((HEAD_WIDTH, span), key_value.dtype),
            jax.ShapeDtypeStruct((8, 128), jnp.float32),
        ],
        cost_estimate=light_cost(key_value),
        name="prepare",
    )(key_value)


def on_device(packed_query_rows, packed_key_rows, packed_value_rows, doc_lengths):
    device_rows = packed_query_rows.shape[0]
    slots = lax.axis_size("kv")
    regions = lax.axis_size("pb")
    span = device_rows * slots
    exchange = lambda array: lax.all_to_all(array, "kv", 0, 0)

    key_value = exchange(pair_slots(packed_key_rows, packed_value_rows, slots))
    queries = [exchange(q).reshape(span, HEAD_WIDTH) for q in query_slots(packed_query_rows, slots)]

    region_first = lax.axis_index("pb") * span
    doc_ends = jnp.cumsum(doc_lengths)
    docs = jnp.concatenate([doc_ends - doc_lengths, doc_ends]) - region_first

    k, vt, norm = prepare(key_value.reshape(span, 2 * HEAD_WIDTH))
    onward = [(i, i + slots) for i in range((regions - 1) * slots)]
    before = [lax.ppermute(array, ("pb", "kv"), onward) for array in (k, vt, norm)]
    largest = jnp.maximum(norm[0, :1], before[2][0, :1])

    results = [
        exchange(
            attend(docs, largest, q, k, vt, before[0], before[1]).reshape(
                slots, device_rows, HEAD_WIDTH
            )
        )
        for q in queries
    ]
    return join(results)


def solution(mesh):
    placed = (P(("pb", "kv"), None), P(("pb", "kv"), None), P(("pb", "kv"), None), P())
    return jax.shard_map(
        on_device, mesh=mesh, in_specs=placed, out_specs=P(("pb", "kv"), None), check_vma=False
    )
```

```python
import functools
import math

import jax
import jax.numpy as jnp
from jax import lax
from jax.experimental import pallas as pl
from jax.experimental.pallas import tpu as pltpu
from jax.sharding import PartitionSpec as P

QUERY_HEADS = 32
KEY_VALUE_HEADS = 8
HEAD_WIDTH = 128
DOCS = 12
CHUNKS = 2
TILE = 2048
STRIP = 256
BLOCK = 128
ROW_COUNTS = (512, 1024, 1536, 2048)
WIDE = 1024
ONES = 16
GROUP = 4
LOG2_SCALE = math.log2(math.e) / math.sqrt(HEAD_WIDTH)
SAFE_EXPONENT = 96.0
LOW = -1e30
MASKED = -3e38
VMEM_LIMIT = 56 * 1024 * 1024


def first_doc(docs_ref, first):
    start, end = docs_ref[0], docs_ref[DOCS]
    for i in range(1, DOCS):
        inside = docs_ref[i] <= first
        start = jnp.where(inside, docs_ref[i], start)
        end = jnp.where(inside, docs_ref[DOCS + i], end)
    return start, end


def values_and_ones(kv_ref, first_key, width):
    half = slice(HEAD_WIDTH, 2 * HEAD_WIDTH)
    blocks = [kv_ref[pl.ds(first_key + i, BLOCK), half] for i in range(0, width, BLOCK)]
    ones = jnp.ones((ONES, width), kv_ref.dtype)
    return jnp.concatenate([jnp.concatenate(blocks, axis=1), ones], axis=0)


def fast_step(qt_ref, kv_ref, acc_ref, rows, first_key, width, allowed=None):
    keys = kv_ref[pl.ds(first_key, width), :HEAD_WIDTH]
    scores = jnp.dot(keys, qt_ref[:, rows], preferred_element_type=jnp.float32)
    weights = jnp.exp2(scores * LOG2_SCALE)
    if allowed is not None:
        weights = jnp.where(allowed, weights, 0.0)
    acc_ref[:, rows] += jnp.dot(
        values_and_ones(kv_ref, first_key, width),
        weights.astype(jnp.bfloat16),
        preferred_element_type=jnp.float32,
    )


def safe_step(qt_ref, kv_ref, acc_ref, max_ref, first_key, width, allowed):
    keys = kv_ref[pl.ds(first_key, width), :HEAD_WIDTH]
    scores = jnp.dot(keys, qt_ref[...], preferred_element_type=jnp.float32)
    scores = jnp.where(allowed, scores * LOG2_SCALE, MASKED)
    old = max_ref[0:1, :]
    new = jnp.maximum(old, jnp.max(scores, axis=0, keepdims=True))
    weights = jnp.exp2(scores - new)
    factor = jnp.exp2(old - new)
    max_ref[...] = jnp.broadcast_to(new, max_ref.shape)
    acc_ref[...] = acc_ref[...] * factor + jnp.dot(
        values_and_ones(kv_ref, first_key, width),
        weights.astype(jnp.bfloat16),
        preferred_element_type=jnp.float32,
    )


def left_keys(qt_ref, kv_ref, acc_ref, start, stop, active):
    low = start // STRIP * STRIP
    strips = (stop - low) // STRIP
    single = (strips - 1) % 2 + 1
    rest = (strips - single) % (WIDE // STRIP)
    wide = (strips - single) // (WIDE // STRIP)
    for fewer, count in zip((0, *ROW_COUNTS), ROW_COUNTS):
        fits = (active > fewer) & (active <= count)

        @pl.when((start < stop) & fits)
        def _():
            rows = slice(0, count)
            place = lax.broadcasted_iota(jnp.int32, (STRIP, count), 0)
            step = functools.partial(fast_step, qt_ref, kv_ref, acc_ref, rows)

            def one_single(i, carry):
                first_key = low + i * STRIP
                step(pl.multiple_of(first_key, STRIP), STRIP, place >= start - first_key)
                return carry

            lax.fori_loop(0, single, one_single, 0)
            size, after = 2, low + single * STRIP
            while size * STRIP < WIDE:
                present = rest // size % 2

                @pl.when(present > 0)
                def _(size=size, after=after):
                    step(pl.multiple_of(after, STRIP), size * STRIP)

                after = after + present * size * STRIP
                size *= 2

            def one_wide(i, carry):
                step(pl.multiple_of(after + i * WIDE, STRIP), WIDE)
                return carry

            lax.fori_loop(0, wide, one_wide, 0)


def row_starts(docs_ref, first):
    position = lax.broadcasted_iota(jnp.int32, (8, TILE), 1) + first
    start = jnp.full((8, TILE), docs_ref[0], jnp.int32)
    for i in range(1, DOCS):
        start = jnp.where(position >= docs_ref[i], docs_ref[i], start)
    return start


def attend_kernel(
    docs_ref, norm_ref, q_ref, kv_own_ref, kv_before_ref, o_ref, qt_ref, kv_ref, acc_ref, max_ref, sems
):
    span = kv_own_ref.shape[0]
    first = pl.program_id(0) * TILE

    @pl.when(pl.program_id(0) == 0)
    def _():
        loads = [
            pltpu.make_async_copy(source, kv_ref.at[pl.ds(i * span, span), :], sems.at[i])
            for i, source in enumerate((kv_before_ref, kv_own_ref))
        ]
        for load in loads:
            load.start()
        for load in loads:
            load.wait()

    start, end = first_doc(docs_ref, first)
    starts = row_starts(docs_ref, first)
    here = first + span
    start_key = jnp.maximum(start + span, 0)
    acc_ref[...] = jnp.zeros_like(acc_ref)
    for block in range(0, TILE, BLOCK):
        qt_ref[:, block : block + BLOCK] = q_ref[block : block + BLOCK, :]
    qt = qt_ref[...].astype(jnp.float32)
    largest = jnp.max(jnp.sum(qt * qt, axis=0, keepdims=True)) * norm_ref[0]
    bounded = largest <= (SAFE_EXPONENT / LOG2_SCALE) ** 2

    @pl.when(bounded)
    def _():
        left_keys(qt_ref, kv_ref, acc_ref, start_key, here, jnp.minimum(end - first, TILE))

        @pl.when((start < first) & (end < first + TILE))
        def _():
            row = lax.broadcasted_iota(jnp.int32, acc_ref.shape, 1) + first
            acc_ref[...] = jnp.where(row < end, acc_ref[...], 0.0)

        for strip in range(TILE // STRIP):
            rows = slice(strip * STRIP, TILE)
            shape = (STRIP, TILE - strip * STRIP)
            place = lax.broadcasted_iota(jnp.int32, shape, 0)
            row = lax.broadcasted_iota(jnp.int32, shape, 1)
            allowed = (place <= row) & (place >= starts[0:1, rows] - (first + strip * STRIP))
            first_key = pl.multiple_of(here + strip * STRIP, STRIP)
            fast_step(qt_ref, kv_ref, acc_ref, rows, first_key, STRIP, allowed)

    @pl.when(jnp.logical_not(bounded))
    def _():
        max_ref[...] = jnp.full_like(max_ref, LOW)

        def one(i, carry):
            first_key = pl.multiple_of(i * STRIP, STRIP)
            place = lax.broadcasted_iota(jnp.int32, (STRIP, TILE), 0) + (first_key - span)
            row = lax.broadcasted_iota(jnp.int32, (STRIP, TILE), 1) + first
            allowed = (place >= starts[0:1, :]) & (place <= row)
            safe_step(qt_ref, kv_ref, acc_ref, max_ref, first_key, STRIP, allowed)
            return carry

        lax.fori_loop(start_key // STRIP, (here + TILE) // STRIP, one, 0)

    result = acc_ref[0:HEAD_WIDTH, :] / acc_ref[HEAD_WIDTH : HEAD_WIDTH + 1, :]
    for block in range(0, TILE, BLOCK):
        o_ref[block : block + BLOCK, :] = result[:, block : block + BLOCK].astype(o_ref.dtype)


def attend(docs, norm, q, kv, kv_before):
    span = q.shape[0]
    tile = pl.BlockSpec((TILE, HEAD_WIDTH), lambda t, *_: (t, 0))
    anywhere = pl.BlockSpec(memory_space=pl.ANY)
    pairs = span * span // 2
    return pl.pallas_call(
        attend_kernel,
        grid_spec=pltpu.PrefetchScalarGridSpec(
            num_scalar_prefetch=2,
            grid=(span // TILE,),
            in_specs=[tile, anywhere, anywhere],
            out_specs=tile,
            scratch_shapes=[
                pltpu.VMEM((HEAD_WIDTH, TILE), jnp.bfloat16),
                pltpu.VMEM((2 * span, 2 * HEAD_WIDTH), jnp.bfloat16),
                pltpu.VMEM((HEAD_WIDTH + ONES, TILE), jnp.float32),
                pltpu.VMEM((8, TILE), jnp.float32),
                pltpu.SemaphoreType.DMA((2,)),
            ],
        ),
        out_shape=jax.ShapeDtypeStruct((span, HEAD_WIDTH), jnp.bfloat16),
        compiler_params=pltpu.CompilerParams(vmem_limit_bytes=VMEM_LIMIT),
        cost_estimate=pl.CostEstimate(
            flops=pairs * 16 * HEAD_WIDTH, bytes_accessed=span * 1536, transcendentals=pairs
        ),
        name="attend",
    )(docs, norm, q, kv, kv_before)


def light_cost(*arrays):
    return pl.CostEstimate(
        flops=0, bytes_accessed=2 * sum(a.size * a.dtype.itemsize for a in arrays), transcendentals=0
    )


def pair_slots_kernel(copies, k_ref, v_ref, o_ref):
    for slot in range(GROUP):
        head = slice(slot // copies * HEAD_WIDTH, (slot // copies + 1) * HEAD_WIDTH)
        o_ref[slot, :, :HEAD_WIDTH] = k_ref[:, head]
        for block in range(0, v_ref.shape[0], BLOCK):
            rows = slice(block, block + BLOCK)
            o_ref[slot, rows, HEAD_WIDTH:] = v_ref[rows, head].T


def pair_slots(k, v, slots):
    rows = k.shape[0]
    copies = slots // KEY_VALUE_HEADS
    part = pl.BlockSpec((rows, GROUP // copies * HEAD_WIDTH), lambda t: (0, t))
    return pl.pallas_call(
        functools.partial(pair_slots_kernel, copies),
        grid=(slots // GROUP,),
        in_specs=[part, part],
        out_specs=pl.BlockSpec((GROUP, rows, 2 * HEAD_WIDTH), lambda t: (t, 0, 0)),
        out_shape=jax.ShapeDtypeStruct((slots, rows, 2 * HEAD_WIDTH), k.dtype),
        cost_estimate=light_cost(k, v),
        name="pair_slots",
    )(k, v)


def query_slots_kernel(q_ref, *o_refs):
    for slot in range(GROUP):
        for c, o_ref in enumerate(o_refs):
            head = slice((slot * CHUNKS + c) * HEAD_WIDTH, (slot * CHUNKS + c + 1) * HEAD_WIDTH)
            for block in range(0, q_ref.shape[0], BLOCK):
                rows = slice(block, block + BLOCK)
                o_ref[slot, rows, :] = q_ref[rows, head].T


def query_slots(q, slots):
    rows = q.shape[0]
    return pl.pallas_call(
        query_slots_kernel,
        grid=(slots // GROUP,),
        in_specs=[pl.BlockSpec((rows, GROUP * CHUNKS * HEAD_WIDTH), lambda t: (0, t))],
        out_specs=[pl.BlockSpec((GROUP, rows, HEAD_WIDTH), lambda t: (t, 0, 0))] * CHUNKS,
        out_shape=[jax.ShapeDtypeStruct((slots, rows, HEAD_WIDTH), q.dtype)] * CHUNKS,
        cost_estimate=pl.CostEstimate(
            flops=q.size * 2 * BLOCK * BLOCK, bytes_accessed=4 * q.size, transcendentals=0
        ),
        name="query_slots",
    )(q)


def join_kernel(*refs):
    *parts, o_ref = refs
    for slot in range(GROUP):
        for c, part in enumerate(parts):
            head = slice((slot * CHUNKS + c) * HEAD_WIDTH, (slot * CHUNKS + c + 1) * HEAD_WIDTH)
            for block in range(0, o_ref.shape[0], BLOCK):
                rows = slice(block, block + BLOCK)
                o_ref[rows, head] = part[slot, rows, :].T


def join(parts):
    slots, rows, _ = parts[0].shape
    return pl.pallas_call(
        join_kernel,
        grid=(slots // GROUP,),
        in_specs=[pl.BlockSpec((GROUP, rows, HEAD_WIDTH), lambda t: (t, 0, 0))] * CHUNKS,
        out_specs=pl.BlockSpec((rows, GROUP * CHUNKS * HEAD_WIDTH), lambda t: (0, t)),
        out_shape=jax.ShapeDtypeStruct((rows, slots * CHUNKS * HEAD_WIDTH), parts[0].dtype),
        cost_estimate=light_cost(*parts),
        name="join",
    )(*parts)


def key_norm_kernel(k_ref, norm_ref):
    kf = k_ref[...].astype(jnp.float32)
    norm = jnp.full(norm_ref.shape, jnp.max(jnp.sum(kf * kf, axis=1, keepdims=True)), jnp.float32)

    @pl.when(pl.program_id(0) == 0)
    def _():
        norm_ref[...] = norm

    @pl.when(pl.program_id(0) > 0)
    def _():
        norm_ref[...] = jnp.maximum(norm_ref[...], norm)


def key_norm(key_value):
    return pl.pallas_call(
        key_norm_kernel,
        grid=(key_value.shape[0] // TILE,),
        in_specs=[pl.BlockSpec((TILE, HEAD_WIDTH), lambda t: (t, 0))],
        out_specs=pl.BlockSpec((8, 128), lambda t: (0, 0)),
        out_shape=jax.ShapeDtypeStruct((8, 128), jnp.float32),
        cost_estimate=light_cost(key_value),
        name="key_norm",
    )(key_value)


def on_device(packed_query_rows, packed_key_rows, packed_value_rows, doc_lengths):
    device_rows = packed_query_rows.shape[0]
    slots = lax.axis_size("kv")
    regions = lax.axis_size("pb")
    span = device_rows * slots
    exchange = lambda array: lax.all_to_all(array, "kv", 0, 0)

    key_value = exchange(pair_slots(packed_key_rows, packed_value_rows, slots))
    parts = query_slots(packed_query_rows, slots)
    queries = [exchange(part).reshape(span, HEAD_WIDTH) for part in parts]

    region_first = lax.axis_index("pb") * span
    doc_ends = jnp.cumsum(doc_lengths)
    docs = jnp.concatenate([doc_ends - doc_lengths, doc_ends]) - region_first

    key_value = key_value.reshape(span, 2 * HEAD_WIDTH)
    norm = key_norm(key_value)
    onward = [(i, i + slots) for i in range((regions - 1) * slots)]
    kv_before, norm_before = [lax.ppermute(array, ("pb", "kv"), onward) for array in (key_value, norm)]
    largest = jnp.maximum(norm[0, :1], norm_before[0, :1])

    results = []
    for q in queries:
        result = attend(docs, largest, q, key_value, kv_before)
        results.append(exchange(result.reshape(slots, device_rows, HEAD_WIDTH)))
    return join(results)


def solution(mesh):
    placed = (P(("pb", "kv"), None), P(("pb", "kv"), None), P(("pb", "kv"), None), P())
    return jax.shard_map(
        on_device, mesh=mesh, in_specs=placed, out_specs=P(("pb", "kv"), None), check_vma=False
    )
```

```python
import functools
import math

import jax
import jax.numpy as jnp
from jax import lax
from jax.experimental import pallas as pl
from jax.experimental.pallas import tpu as pltpu
from jax.sharding import PartitionSpec as P

QUERY_HEADS = 32
KEY_VALUE_HEADS = 8
HEAD_WIDTH = 128
DOCS = 12
CHUNKS = 2
TILE = 2048
STRIP = 256
BLOCK = 128
ROW_COUNTS = (512, 1024, 1536, 2048)
WIDE = 1024
ONES = 16
NORM_ROWS = 16
NORM_MARGIN = 1.01
GROUP = 8
LOG2_SCALE = math.log2(math.e) / math.sqrt(HEAD_WIDTH)
SAFE_EXPONENT = 96.0
LOW = -1e30
MASKED = -3e38
VMEM_LIMIT = 56 * 1024 * 1024


def first_doc(docs_ref, first):
    start, end = docs_ref[0], docs_ref[DOCS]
    for i in range(1, DOCS):
        inside = docs_ref[i] <= first
        start = jnp.where(inside, docs_ref[i], start)
        end = jnp.where(inside, docs_ref[DOCS + i], end)
    return start, end


def values_and_ones(kv_ref, first_key, width):
    half = slice(HEAD_WIDTH, 2 * HEAD_WIDTH)
    blocks = [kv_ref[pl.ds(first_key + i, BLOCK), half] for i in range(0, width, BLOCK)]
    ones = jnp.ones((ONES, width), kv_ref.dtype)
    return jnp.concatenate([jnp.concatenate(blocks, axis=1), ones], axis=0)


def fast_step(qt_ref, kv_ref, acc_ref, rows, first_key, width, allowed=None, kept=None):
    keys = kv_ref[pl.ds(first_key, width), :HEAD_WIDTH]
    scores = jnp.dot(keys, qt_ref[:, rows], preferred_element_type=jnp.float32)
    weights = jnp.exp2(scores * LOG2_SCALE)
    if allowed is not None:
        weights = jnp.where(allowed, weights, 0.0)
    update = jnp.dot(
        values_and_ones(kv_ref, first_key, width),
        weights.astype(jnp.bfloat16),
        preferred_element_type=jnp.float32,
    )
    acc_ref[:, rows] += update if kept is None else jnp.where(kept, update, 0.0)


def safe_step(qt_ref, kv_ref, acc_ref, max_ref, first_key, width, allowed):
    keys = kv_ref[pl.ds(first_key, width), :HEAD_WIDTH]
    scores = jnp.dot(keys, qt_ref[...], preferred_element_type=jnp.float32)
    scores = jnp.where(allowed, scores * LOG2_SCALE, MASKED)
    old = max_ref[0:1, :]
    new = jnp.maximum(old, jnp.max(scores, axis=0, keepdims=True))
    weights = jnp.exp2(scores - new)
    factor = jnp.exp2(old - new)
    max_ref[...] = jnp.broadcast_to(new, max_ref.shape)
    acc_ref[...] = acc_ref[...] * factor + jnp.dot(
        values_and_ones(kv_ref, first_key, width),
        weights.astype(jnp.bfloat16),
        preferred_element_type=jnp.float32,
    )


def left_keys(qt_ref, kv_ref, acc_ref, start, stop, active):
    low = start // STRIP * STRIP
    strips = (stop - low) // STRIP
    single = (strips - 1) % 2 + 1
    rest = (strips - single) % (WIDE // STRIP)
    wide = (strips - single) // (WIDE // STRIP)
    for fewer, count in zip((0, *ROW_COUNTS), ROW_COUNTS):
        fits = (active > fewer) & (active <= count)

        @pl.when((start < stop) & fits)
        def _():
            rows = slice(0, count)
            place = lax.broadcasted_iota(jnp.int32, (STRIP, count), 0)
            kept = lax.broadcasted_iota(jnp.int32, (HEAD_WIDTH + ONES, count), 1) < active
            step = functools.partial(fast_step, qt_ref, kv_ref, acc_ref, rows, kept=kept)

            def one_single(i, carry):
                first_key = low + i * STRIP
                step(pl.multiple_of(first_key, STRIP), STRIP, place >= start - first_key)
                return carry

            lax.fori_loop(0, single, one_single, 0)
            size, after = 2, low + single * STRIP
            while size * STRIP < WIDE:
                present = rest // size % 2

                @pl.when(present > 0)
                def _(size=size, after=after):
                    step(pl.multiple_of(after, STRIP), size * STRIP)

                after = after + present * size * STRIP
                size *= 2

            def one_wide(i, carry):
                step(pl.multiple_of(after + i * WIDE, STRIP), WIDE)
                return carry

            lax.fori_loop(0, wide, one_wide, 0)


def row_starts(docs_ref, first):
    position = lax.broadcasted_iota(jnp.int32, (8, TILE), 1) + first
    start = jnp.full((8, TILE), docs_ref[0], jnp.int32)
    for i in range(1, DOCS):
        start = jnp.where(position >= docs_ref[i], docs_ref[i], start)
    return start


def attend_kernel(
    docs_ref, q_ref, own_ref, before_ref, o_ref, qt_ref, kv_ref, norm_ref, acc_ref, max_ref, largest_ref,
    piece_sems, norm_sems,
):
    slots = own_ref.shape[0]
    rows_each = own_ref.shape[1] - NORM_ROWS
    span = slots * rows_each
    tile = pl.program_id(0)
    first = tile * TILE

    def piece(i, slot):
        source = (before_ref, own_ref)[i].at[slot, pl.ds(0, rows_each), :]
        place = pl.ds(i * span + slot * rows_each, rows_each)
        return pltpu.make_async_copy(source, kv_ref.at[place, :], piece_sems.at[i, slot])

    def norms(i):
        source = (before_ref, own_ref)[i].at[:, pl.ds(rows_each, NORM_ROWS), :]
        return pltpu.make_async_copy(source, norm_ref.at[i], norm_sems.at[i])

    @pl.when(tile == 0)
    def _():
        for i in (1, 0):
            norms(i).start()
        for i in (1, 0):
            for slot in range(slots):
                piece(i, slot).start()
        for i in (1, 0):
            norms(i).wait()
        largest_ref[0] = jnp.max(norm_ref[...].astype(jnp.float32))

    ready = [-(-(t * TILE) // rows_each) for t in range(span // TILE + 1)]
    for t in range(span // TILE):

        @pl.when(tile == t)
        def _():
            for slot in range(ready[t], ready[t + 1]):
                piece(1, slot).wait()

    start, end = first_doc(docs_ref, first)
    starts = row_starts(docs_ref, first)
    here = first + span
    start_key = jnp.maximum(start + span, 0)
    acc_ref[...] = jnp.zeros_like(acc_ref)
    for block in range(0, TILE, BLOCK):
        qt_ref[:, block : block + BLOCK] = q_ref[block : block + BLOCK, :]
    qt = qt_ref[...].astype(jnp.float32)
    largest = jnp.max(jnp.sum(qt * qt, axis=0, keepdims=True)) * largest_ref[0]
    bounded = largest <= (SAFE_EXPONENT / LOG2_SCALE) ** 2

    @pl.when(bounded)
    def _():
        for strip in range(TILE // STRIP):
            rows = slice(strip * STRIP, TILE)
            shape = (STRIP, TILE - strip * STRIP)
            place = lax.broadcasted_iota(jnp.int32, shape, 0)
            row = lax.broadcasted_iota(jnp.int32, shape, 1)
            allowed = (place <= row) & (place >= starts[0:1, rows] - (first + strip * STRIP))
            first_key = pl.multiple_of(here + strip * STRIP, STRIP)
            fast_step(qt_ref, kv_ref, acc_ref, rows, first_key, STRIP, allowed)

    @pl.when(tile == 0)
    def _():
        for slot in range(slots):
            piece(0, slot).wait()

    @pl.when(bounded)
    def _():
        left_keys(qt_ref, kv_ref, acc_ref, start_key, here, jnp.minimum(end - first, TILE))

    @pl.when(jnp.logical_not(bounded))
    def _():
        max_ref[...] = jnp.full_like(max_ref, LOW)

        def one(i, carry):
            first_key = pl.multiple_of(i * STRIP, STRIP)
            place = lax.broadcasted_iota(jnp.int32, (STRIP, TILE), 0) + (first_key - span)
            row = lax.broadcasted_iota(jnp.int32, (STRIP, TILE), 1) + first
            allowed = (place >= starts[0:1, :]) & (place <= row)
            safe_step(qt_ref, kv_ref, acc_ref, max_ref, first_key, STRIP, allowed)
            return carry

        lax.fori_loop(start_key // STRIP, (here + TILE) // STRIP, one, 0)

    result = acc_ref[0:HEAD_WIDTH, :] / acc_ref[HEAD_WIDTH : HEAD_WIDTH + 1, :]
    for block in range(0, TILE, BLOCK):
        o_ref[block : block + BLOCK, :] = result[:, block : block + BLOCK].astype(o_ref.dtype)


def attend(docs, q, kv, kv_before):
    span = q.shape[0]
    tile = pl.BlockSpec((TILE, HEAD_WIDTH), lambda t, *_: (t, 0))
    anywhere = pl.BlockSpec(memory_space=pl.ANY)
    pairs = span * span // 2
    return pl.pallas_call(
        attend_kernel,
        grid_spec=pltpu.PrefetchScalarGridSpec(
            num_scalar_prefetch=1,
            grid=(span // TILE,),
            in_specs=[tile, anywhere, anywhere],
            out_specs=tile,
            scratch_shapes=[
                pltpu.VMEM((HEAD_WIDTH, TILE), jnp.bfloat16),
                pltpu.VMEM((2 * span, 2 * HEAD_WIDTH), jnp.bfloat16),
                pltpu.VMEM((2, kv.shape[0], NORM_ROWS, 2 * HEAD_WIDTH), jnp.bfloat16),
                pltpu.VMEM((HEAD_WIDTH + ONES, TILE), jnp.float32),
                pltpu.VMEM((8, TILE), jnp.float32),
                pltpu.SMEM((1,), jnp.float32),
                pltpu.SemaphoreType.DMA((2, kv.shape[0])),
                pltpu.SemaphoreType.DMA((2,)),
            ],
        ),
        out_shape=jax.ShapeDtypeStruct((span, HEAD_WIDTH), jnp.bfloat16),
        compiler_params=pltpu.CompilerParams(vmem_limit_bytes=VMEM_LIMIT),
        cost_estimate=pl.CostEstimate(
            flops=pairs * 16 * HEAD_WIDTH, bytes_accessed=span * 1536, transcendentals=pairs
        ),
        name="attend",
    )(docs, q, kv, kv_before)


def light_cost(*arrays):
    return pl.CostEstimate(
        flops=0, bytes_accessed=2 * sum(a.size * a.dtype.itemsize for a in arrays), transcendentals=0
    )


def pair_slots_kernel(copies, k_ref, v_ref, o_ref):
    rows_each = k_ref.shape[0]
    for slot in range(GROUP):
        head = slice(slot // copies * HEAD_WIDTH, (slot // copies + 1) * HEAD_WIDTH)
        keys = k_ref[:, head]
        o_ref[slot, :rows_each, :HEAD_WIDTH] = keys
        for block in range(0, rows_each, BLOCK):
            rows = slice(block, block + BLOCK)
            o_ref[slot, rows, HEAD_WIDTH:] = v_ref[rows, head].T
        squares = jnp.square(keys.astype(jnp.float32))
        norm = jnp.max(jnp.sum(squares, axis=1, keepdims=True)) * NORM_MARGIN
        filled = jnp.full((NORM_ROWS, 2 * HEAD_WIDTH), norm, jnp.float32)
        o_ref[slot, rows_each:, :] = filled.astype(o_ref.dtype)


def pair_slots(k, v, slots):
    rows = k.shape[0]
    copies = slots // KEY_VALUE_HEADS
    part = pl.BlockSpec((rows, GROUP // copies * HEAD_WIDTH), lambda t: (0, t))
    shape = (GROUP, rows + NORM_ROWS, 2 * HEAD_WIDTH)
    return pl.pallas_call(
        functools.partial(pair_slots_kernel, copies),
        grid=(slots // GROUP,),
        in_specs=[part, part],
        out_specs=pl.BlockSpec(shape, lambda t: (t, 0, 0)),
        out_shape=jax.ShapeDtypeStruct((slots, *shape[1:]), k.dtype),
        cost_estimate=light_cost(k, v),
        name="pair_slots",
    )(k, v)


def query_slots_kernel(q_ref, *o_refs):
    for slot in range(GROUP):
        for c, o_ref in enumerate(o_refs):
            head = slice((slot * CHUNKS + c) * HEAD_WIDTH, (slot * CHUNKS + c + 1) * HEAD_WIDTH)
            for block in range(0, q_ref.shape[0], BLOCK):
                rows = slice(block, block + BLOCK)
                o_ref[slot, rows, :] = q_ref[rows, head].T


def query_slots(q, slots):
    rows = q.shape[0]
    return pl.pallas_call(
        query_slots_kernel,
        grid=(slots // GROUP,),
        in_specs=[pl.BlockSpec((rows, GROUP * CHUNKS * HEAD_WIDTH), lambda t: (0, t))],
        out_specs=[pl.BlockSpec((GROUP, rows, HEAD_WIDTH), lambda t: (t, 0, 0))] * CHUNKS,
        out_shape=[jax.ShapeDtypeStruct((slots, rows, HEAD_WIDTH), q.dtype)] * CHUNKS,
        cost_estimate=pl.CostEstimate(
            flops=q.size * 2 * BLOCK * BLOCK, bytes_accessed=4 * q.size, transcendentals=0
        ),
        name="query_slots",
    )(q)


def join_kernel(*refs):
    *parts, o_ref = refs
    for slot in range(GROUP):
        for c, part in enumerate(parts):
            head = slice((slot * CHUNKS + c) * HEAD_WIDTH, (slot * CHUNKS + c + 1) * HEAD_WIDTH)
            for block in range(0, o_ref.shape[0], BLOCK):
                rows = slice(block, block + BLOCK)
                o_ref[rows, head] = part[slot, rows, :].T


def join(parts):
    slots, rows, _ = parts[0].shape
    return pl.pallas_call(
        join_kernel,
        grid=(slots // GROUP,),
        in_specs=[pl.BlockSpec((GROUP, rows, HEAD_WIDTH), lambda t: (t, 0, 0))] * CHUNKS,
        out_specs=pl.BlockSpec((rows, GROUP * CHUNKS * HEAD_WIDTH), lambda t: (0, t)),
        out_shape=jax.ShapeDtypeStruct((rows, slots * CHUNKS * HEAD_WIDTH), parts[0].dtype),
        cost_estimate=light_cost(*parts),
        name="join",
    )(*parts)


def on_device(packed_query_rows, packed_key_rows, packed_value_rows, doc_lengths):
    device_rows = packed_query_rows.shape[0]
    slots = lax.axis_size("kv")
    regions = lax.axis_size("pb")
    span = device_rows * slots
    exchange = lambda array: lax.all_to_all(array, "kv", 0, 0)

    key_value = exchange(pair_slots(packed_key_rows, packed_value_rows, slots))
    parts = query_slots(packed_query_rows, slots)
    queries = [exchange(part).reshape(span, HEAD_WIDTH) for part in parts]

    region_first = lax.axis_index("pb") * span
    doc_ends = jnp.cumsum(doc_lengths)
    docs = jnp.concatenate([doc_ends - doc_lengths, doc_ends]) - region_first

    onward = [(i, i + slots) for i in range((regions - 1) * slots)]
    kv_before = lax.ppermute(key_value, ("pb", "kv"), onward)

    results = []
    for q in queries:
        result = attend(docs, q, key_value, kv_before)
        results.append(exchange(result.reshape(slots, device_rows, HEAD_WIDTH)))
    return join(results)


def solution(mesh):
    placed = (P(("pb", "kv"), None), P(("pb", "kv"), None), P(("pb", "kv"), None), P())
    return jax.shard_map(
        on_device, mesh=mesh, in_specs=placed, out_specs=P(("pb", "kv"), None), check_vma=False
    )
```
